128 devices in a mesh: attn: 8 (over y, core), exp: 16 (over x, z).
Axes of the slice: x: 4, y: 4, z: 4, core: 2. Of those that a mesh axis runs over, the one named last changes fastest.
Arguments:
- moe_in: bfloat16 [768, 7168], P(('attn', 'exp')), may hold values from -6 to 6
- routes: int32 [768, 2], P(('attn', 'exp')), may hold values from 0 to 15, all different within a row; in each aligned block of 6 rows (0 to 5, 6 to 11, ...) at most 2 rows name the same one
- gates: float32 [768, 2], P(('attn', 'exp')), may hold values from 0.2 to 1
- gate_w: bfloat16 [16, 7168, 2048], P('exp', None, 'attn'), may hold values from -0.0625 to 0.0625
- up_w: bfloat16 [16, 7168, 2048], P('exp', None, 'attn'), may hold values from -0.0625 to 0.0625
- down_w: bfloat16 [16, 2048, 7168], P('exp', 'attn'), may hold values from -0.125 to 0.125
- queries: bfloat16 [512, 128, 576], P(('attn', 'exp')), may hold values from -55 to 55
- latent_cache: bfloat16 [512, 2048, 576], P(('attn', 'exp')), may hold values from -4 to 4
- lengths: int32 [512], P(('attn', 'exp')), may hold values from 2 to 2048, as said below
Outputs:
- moe_out: bfloat16 [768, 7168], P(('attn', 'exp'))
- attended: bfloat16 [512, 128, 512], P(('attn', 'exp'))
The draws below stay inside these ranges and needn't reach their ends.
Inputs may be any that keep to these rules, and one draw needn't show every extreme that they name: `routes`: each row names 2 different experts; among the rows of one device no expert is named more than 2 times, and in every draw some expert is named exactly 2 times by the rows of some device. Row r attends to cache positions below lengths[r]; some row has all 2048.
All inputs are finite; a program needn't handle non-finite values.
Results may differ from the reference program's by a relative error of at most 0.015.
Values may be sent and summed in bfloat16 or wider, within the bound.
No kernel may reach another device: no remote copies, remote signals or barrier semaphores. Data moves between devices by JAX's collectives and lax.ppermute only.
A program may use at most 128 MiB of HBM per device.

```python
import math
import jax
import jax.numpy as jnp
import numpy as np
from jax import lax

D = 7168
FF = 2048
H = 128
KV = 512
TOPK = 2
ROWS_DEV = 6
CTX = 2048
QK = 576
EXPERTS = 16
CAP = 2
ROWS = 768
AROWS = 512
N_ATTN = 8


def draw_queries(key, part):
    key = jax.random.fold_in(key, 1)
    values = jnp.clip(jax.random.normal(key, (AROWS, H, QK), jnp.float32), -4.0, 4.0)
    return values.astype(jnp.bfloat16)


def draw_latent_cache(key, part):
    key = jax.random.fold_in(key, 2)
    values = jnp.clip(jax.random.normal(key, (AROWS, CTX, QK), jnp.float32), -4.0, 4.0)
    return values.astype(jnp.bfloat16)


def draw_lengths(key, part):
    key = jax.random.fold_in(key, 3)
    drawn = jax.random.randint(key, (AROWS,), 2, CTX + 1, dtype=jnp.int32)
    return drawn.at[0].set(CTX)


def block_levels(key, extent, shards, least, top_value):
    level = 1.0
    for axis_at, blocks in shards:
        draws = jax.random.uniform(jax.random.fold_in(jax.random.fold_in(key, 6), axis_at), (blocks,), jnp.float32, least / len(shards), top_value / len(shards))
        level = level * jnp.repeat(jnp.exp(draws), extent[axis_at] // blocks).reshape((-1,) + (1,) * (len(extent) - 1 - axis_at))
    return level


def routed_block(rng, own, number, rows, count, top, limit, lean):
    order = jax.random.permutation(rng, count)
    packed, common = portions_of(count, rows * top, limit, lean, True), portions_of(count, rows * top, limit, lean, False)
    places = jnp.arange(count)

    def named(sizes, rotation):
        used = int((sizes > 0).sum())
        fixed = max(1, used // 4)
        passed = fixed + (places - fixed + rotation * (used - fixed)) % max(1, count - fixed)
        return jnp.zeros((count,), jnp.int32).at[order[jnp.where(places < fixed, places, passed)]].set(jnp.asarray(sizes, jnp.int32))

    sizes = jnp.where(number % 4 == 0, named(packed, number // 4), named(common, number - number // 4 - 1))
    mixed = jax.random.permutation(jax.random.fold_in(own, 3), count)
    donor, sink = mixed[0:count // 2 * 2:2], mixed[1:count // 2 * 2:2]
    room = jnp.minimum(sizes[donor] - 1, limit - sizes[sink]) // 2
    room = jnp.where((donor == order[0]) | (sink == order[0]) | (sizes[sink] == 0), 0, jnp.maximum(room, 0))
    passed = jax.random.randint(jax.random.fold_in(own, 4), (count // 2,), 0, 1 << 20) % (room + 1)
    sizes = sizes.at[donor].add(-passed).at[sink].add(passed)
    labels = jnp.searchsorted(jnp.cumsum(sizes), jnp.arange(rows * top), side="right").astype(jnp.int32)
    listing = labels.reshape(top, rows).T
    listing = listing[jax.random.permutation(jax.random.fold_in(own, 1), rows)]
    rotation = jax.random.randint(jax.random.fold_in(own, 2), (rows, 1), 0, top)
    return jnp.take_along_axis(listing, (jnp.arange(top)[None, :] + rotation) % top, axis=1)


def portions_of(number_of, total, bound, skew, full):
    loads = [(1 << 20) // math.isqrt(standing ** skew) + 1 for standing in range(1, number_of + 1)]
    largest = bound if full else min(bound, max(-(-total // number_of), total * loads[0] // sum(loads)))
    least = 1 if total - largest >= number_of - 1 else 0
    counts, spare = [largest] + [least] * (number_of - 1), total - largest - least * (number_of - 1)
    while spare > 0:
        free = [i for i in range(1, number_of) if counts[i] < largest] or [i for i in range(1, number_of) if counts[i] < bound]
        pool, remaining = sum([loads[i] for i in free]), spare
        for i in free:
            addition = min(bound - counts[i], max(1, remaining * loads[i] // pool), spare)
            counts[i] = counts[i] + addition
            spare = spare - addition
    return np.array(counts)


def scatter_about(rng, shape, scale, most, split=(), kind=jnp.bfloat16):
    array = jax.random.normal(rng, shape, jnp.float32) * scale
    if len(split) > 0:
        array = block_levels(rng, shape, split, -0.22, 0.18) * array
    return jnp.clip(array, min=-most, max=most).astype(kind)


def setup_inputs(seed: int = 0) -> dict:
    key_list = jax.random.split(jax.random.key(seed), 10)
    moe_in = scatter_about(key_list[0], (ROWS, D), 1.0, 6.0, ((0, 128),))
    routes_keys = jax.random.split(jax.random.fold_in(key_list[1], 1), ROWS // ROWS_DEV)
    routes_turns = jax.random.permutation(jax.random.fold_in(key_list[1], 3), ROWS // ROWS_DEV)
    routes = jax.vmap(lambda own, number: routed_block(jax.random.fold_in(key_list[1], 2), own, number, ROWS_DEV, EXPERTS, TOPK, CAP, 2))(routes_keys, routes_turns).reshape((ROWS, TOPK))
    gates = jnp.clip(jnp.exp(math.log(1.0) - 1.609438 * jax.random.uniform(key_list[2], (ROWS, TOPK), jnp.float32) ** block_levels(key_list[2], (ROWS, TOPK), ((0, 128),), -0.2, 0.2)), 0.2, 1.0)
    gate_w = scatter_about(key_list[3], (EXPERTS, D, FF), D ** -0.5, 0.0625, ((0, 16), (2, 8)))
    up_w = scatter_about(key_list[4], (EXPERTS, D, FF), D ** -0.5, 0.0625, ((0, 16), (2, 8)))
    down_w = scatter_about(key_list[5], (EXPERTS, FF, D), FF ** -0.5, 0.125, ((0, 16), (1, 8)))
    queries = draw_queries(jax.random.fold_in(key_list[9], 71), 0)
    latent_cache = draw_latent_cache(jax.random.fold_in(key_list[9], 71), 0)
    lengths = draw_lengths(jax.random.fold_in(key_list[9], 71), 0)
    return {"moe_in": moe_in, "routes": routes, "gates": gates, "gate_w": gate_w, "up_w": up_w, "down_w": down_w, "queries": queries, "latent_cache": latent_cache, "lengths": lengths}


score_scale = 192.0 ** -0.5


def attend_row(inputs):
    query, cache, length = inputs
    scores = jnp.dot(query, cache.T, preferred_element_type=jnp.float32) * score_scale
    visible = jnp.arange(CTX, dtype=jnp.int32)[None, :] < length
    scores = jnp.where(visible, scores, -1e30)
    row_max = jnp.max(scores, axis=1, keepdims=True)
    exp_scores = jnp.where(visible, jnp.exp(scores - row_max), 0.0)
    probs = (exp_scores / jnp.sum(exp_scores, axis=1, keepdims=True)).astype(jnp.bfloat16)
    return jnp.dot(probs, cache[:, :KV], preferred_element_type=jnp.float32).astype(jnp.bfloat16)


def reference(moe_in, routes, gates, gate_w, up_w, down_w, queries, latent_cache, lengths):
    attended = lax.map(attend_row, (queries, latent_cache, lengths))
    blocks = ROWS // ROWS_DEV
    route_blocks = routes.reshape(blocks, ROWS_DEV * TOPK)
    one_hot = (route_blocks[:, :, None] == jnp.arange(EXPERTS, dtype=jnp.int32)[None, None, :]).astype(jnp.int32)
    earlier = jnp.cumsum(one_hot, axis=1) - one_hot
    slot_ids = jnp.sum(earlier * one_hot, axis=2).astype(jnp.int32)
    row_ids = (jnp.arange(ROWS * TOPK, dtype=jnp.int32) // TOPK).reshape(blocks, ROWS_DEV * TOPK)
    block_ids = jnp.broadcast_to(jnp.arange(blocks, dtype=jnp.int32)[:, None], route_blocks.shape)
    table = jnp.full((EXPERTS, blocks, CAP), ROWS, jnp.int32).at[route_blocks, block_ids, slot_ids].set(row_ids)
    padded = jnp.concatenate([moe_in, jnp.zeros((1, D), jnp.bfloat16)], axis=0)
    slice_width = FF // N_ATTN
    total_slots = blocks * CAP

    def expert(index):
        chosen = padded[table[index].reshape(-1)]
        gate_act = jnp.dot(chosen, gate_w[index], preferred_element_type=jnp.float32)
        up_act = jnp.dot(chosen, up_w[index], preferred_element_type=jnp.float32)
        hidden = (jax.nn.silu(gate_act) * up_act).astype(jnp.bfloat16)
        parts = jnp.einsum("mak,akd->amd",
                           hidden.reshape(total_slots, N_ATTN, slice_width).astype(jnp.float32),
                           down_w[index].reshape(N_ATTN, slice_width, D).astype(jnp.float32),
                           precision=lax.Precision.HIGHEST)
        rounded = lax.optimization_barrier(parts.astype(jnp.bfloat16))
        return jnp.sum(rounded.astype(jnp.float32), axis=0).astype(jnp.bfloat16)

    outputs = lax.map(expert, jnp.arange(EXPERTS, dtype=jnp.int32))
    owner_block = (jnp.arange(ROWS, dtype=jnp.int32) // ROWS_DEV)[:, None]
    flat_index = routes * total_slots + owner_block * CAP + slot_ids.reshape(ROWS, TOPK)
    picked = outputs.reshape(EXPERTS * total_slots, D)[flat_index]
    moe_out = jnp.sum(picked.astype(jnp.float32) * gates[:, :, None], axis=1).astype(jnp.bfloat16)
    return moe_out, attended
```

```python
import jax
import jax.numpy as jnp
from jax import lax
from jax.sharding import Mesh, PartitionSpec as P

KV = 512


score_scale = 192.0 ** (-0.5)


def attend(queries, latent_cache, lengths):
    scores = (
        jnp.einsum("rhq,rtq->rht", queries, latent_cache, preferred_element_type=jnp.float32)
        * score_scale
    )
    position = jnp.arange(latent_cache.shape[1], dtype=jnp.int32)
    visible = position[None, None, :] < lengths[:, None, None]
    scores = jnp.where(visible, scores, -1e30)
    row_max = jnp.max(scores, axis=2, keepdims=True)
    exp_scores = jnp.where(visible, jnp.exp(scores - row_max), 0.0)
    probs = (exp_scores / jnp.sum(exp_scores, axis=2, keepdims=True)).astype(jnp.bfloat16)
    values = latent_cache[:, :, :KV]
    return jnp.einsum("rht,rtv->rhv", probs, values, preferred_element_type=jnp.float32).astype(
        jnp.bfloat16
    )


def expert_slice(rows, gate_w, up_w, down_w):
    shape = rows.shape
    rows = rows.reshape(-1, shape[-1])
    gate_act = jnp.dot(rows, gate_w, preferred_element_type=jnp.float32)
    up_act = jnp.dot(rows, up_w, preferred_element_type=jnp.float32)
    hidden = (jax.nn.silu(gate_act) * up_act).astype(jnp.bfloat16)
    out = jnp.dot(hidden, down_w, preferred_element_type=jnp.float32)
    return out.astype(jnp.bfloat16).reshape(shape)


def body(moe_in, routes, gates, gate_w, up_w, down_w, queries, latent_cache, lengths):
    rows_here, top_count = routes.shape
    experts = lax.axis_size("x") * lax.axis_size("z")
    columns = lax.axis_size("y")
    chips = ("y", "x", "z")
    width = moe_in.shape[1]
    capacity = 2
    flat_routes = routes.reshape(-1)
    one_hot = (flat_routes[:, None] == jnp.arange(experts, dtype=jnp.int32)[None, :]).astype(
        jnp.int32
    )
    earlier = jnp.cumsum(one_hot, axis=0) - one_hot
    slot_ids = jnp.sum(earlier * one_hot, axis=1)
    targets = (flat_routes * capacity + slot_ids).reshape(rows_here, top_count)
    places = jnp.arange(capacity * experts, dtype=jnp.int32)
    named = targets[:, :, None] == places[None, None, :]
    selector = jnp.sum(named.astype(jnp.float32), axis=1).astype(jnp.bfloat16)
    outgoing = jnp.dot(selector.T, moe_in, preferred_element_type=jnp.float32).astype(jnp.bfloat16)
    outgoing = outgoing.reshape(1, experts, capacity, width)
    outgoing = jnp.broadcast_to(outgoing, (columns, experts, capacity, width))
    outgoing = outgoing.reshape(columns * experts, capacity, width)
    mine = lax.all_to_all(outgoing, chips, split_axis=0, concat_axis=0, tiled=True)
    swap = [(0, 1), (1, 0)]
    theirs = lax.ppermute(mine, "core", swap)
    weights = (gate_w[0], up_w[0], down_w[0])
    part_mine = expert_slice(mine, *weights)
    part_theirs = expert_slice(theirs, *weights)
    part_back = lax.ppermute(part_theirs, "core", swap)
    summed = (part_mine.astype(jnp.float32) + part_back.astype(jnp.float32)).astype(jnp.bfloat16)
    returned = lax.all_to_all(summed, chips, split_axis=0, concat_axis=0, tiled=True)
    attended = attend(queries, latent_cache, lengths)
    weight = jnp.sum(jnp.where(named, gates[:, :, None], 0.0), axis=1)
    weight = jnp.tile(weight, (1, columns))
    high = weight.astype(jnp.bfloat16)
    low = (weight - high.astype(jnp.float32)).astype(jnp.bfloat16)
    returned = returned.reshape(-1, width)
    moe_out = jnp.dot(high, returned, preferred_element_type=jnp.float32) + jnp.dot(
        low, returned, preferred_element_type=jnp.float32
    )
    return (moe_out.astype(jnp.bfloat16), attended)


def solution(mesh):
    devices = mesh.devices
    split = Mesh(devices.reshape(devices.shape[0] // 2, 2, 4, 4), ("y", "core", "x", "z"))
    attn, exp = ("y", "core"), ("x", "z")
    both = attn + exp
    placed = (
        P(both, None),
        P(both, None),
        P(both, None),
        P(exp, None, attn),
        P(exp, None, attn),
        P(exp, attn, None),
        P(both, None, None),
        P(both, None, None),
        P(both),
    )
    return jax.shard_map(
        body,
        mesh=split,
        in_specs=placed,
        out_specs=(P(both, None), P(both, None, None)),
        check_vma=False,
    )
```

```python
import jax
import jax.numpy as jnp
from jax import lax
from jax.experimental import pallas as pl
from jax.experimental.pallas import tpu as pltpu
from jax.sharding import Mesh, PartitionSpec as P

KV = 512


score_scale = 192.0 ** (-0.5)


def attend(queries, latent_cache, lengths):
    scores = (
        jnp.einsum("rhq,rtq->rht", queries, latent_cache, preferred_element_type=jnp.float32)
        * score_scale
    )
    position = jnp.arange(latent_cache.shape[1], dtype=jnp.int32)
    visible = position[None, None, :] < lengths[:, None, None]
    scores = jnp.where(visible, scores, -1e30)
    row_max = jnp.max(scores, axis=2, keepdims=True)
    exp_scores = jnp.where(visible, jnp.exp(scores - row_max), 0.0)
    probs = (exp_scores / jnp.sum(exp_scores, axis=2, keepdims=True)).astype(jnp.bfloat16)
    values = latent_cache[:, :, :KV]
    return jnp.einsum("rht,rtv->rhv", probs, values, preferred_element_type=jnp.float32).astype(
        jnp.bfloat16
    )


STEPS = 7


def expert_kernel(*refs):
    blocks, refs = refs[:8], refs[8:]
    gate_hbm, up_hbm, down_hbm, theirs_ref, mine_ref = refs[:5]
    gate_buf, up_buf, down_buf, gate_acc, up_acc, sems = refs[5:]
    depth = gate_hbm.shape[1] // STEPS

    def part(step):
        return pl.ds(step * depth, depth)

    def gate_copy(step):
        return pltpu.make_async_copy(
            gate_hbm.at[0, part(step), :], gate_buf.at[part(step), :], sems.at[0, step]
        )

    def up_copy(step):
        return pltpu.make_async_copy(
            up_hbm.at[0, part(step), :], up_buf.at[part(step), :], sems.at[1, step]
        )

    def down_copy(step):
        return pltpu.make_async_copy(
            down_hbm.at[0, :, part(step)], down_buf.at[:, part(step)], sems.at[2, step]
        )

    for step in range(STEPS):
        gate_copy(step).start()
        up_copy(step).start()
    for step in range(STEPS):
        down_copy(step).start()
    for step in range(STEPS):
        rows = jnp.concatenate([b[:, part(step)] for b in blocks], axis=0)
        gate_copy(step).wait()
        gate_act = jnp.dot(rows, gate_buf[part(step), :], preferred_element_type=jnp.float32)
        up_copy(step).wait()
        up_act = jnp.dot(rows, up_buf[part(step), :], preferred_element_type=jnp.float32)
        if step == 0:
            gate_acc[...] = gate_act
            up_acc[...] = up_act
        else:
            gate_acc[...] += gate_act
            up_acc[...] += up_act
    gate_act = gate_acc[...]
    hidden = (gate_act / (1.0 + jnp.exp(-gate_act)) * up_acc[...]).astype(jnp.bfloat16)
    half = hidden.shape[0] // 2
    for step in range(STEPS):
        down_copy(step).wait()
        out = jnp.dot(hidden, down_buf[:, part(step)], preferred_element_type=jnp.float32)
        out = out.astype(jnp.bfloat16)
        theirs_ref[:, part(step)] = out[:half]
        mine_ref[:, part(step)] = out[half:]


def experts_on(theirs, mine, gate_w, up_w, down_w):
    rows, width = mine[0].shape
    hidden = gate_w.shape[2]
    half = jax.ShapeDtypeStruct((len(mine) * rows, width), jnp.bfloat16)
    total = 2 * len(mine) * rows
    whole = pl.BlockSpec(memory_space=pltpu.VMEM)
    return pl.pallas_call(
        expert_kernel,
        out_shape=(half, half),
        in_specs=[whole] * 8 + [pl.BlockSpec(memory_space=pl.ANY)] * 3,
        out_specs=(whole, whole),
        scratch_shapes=[
            pltpu.VMEM((width, hidden), jnp.bfloat16),
            pltpu.VMEM((width, hidden), jnp.bfloat16),
            pltpu.VMEM((hidden, width), jnp.bfloat16),
            pltpu.VMEM((total, hidden), jnp.float32),
            pltpu.VMEM((total, hidden), jnp.float32),
            pltpu.SemaphoreType.DMA((3, STEPS)),
        ],
        compiler_params=pltpu.CompilerParams(vmem_limit_bytes=40 * 2**20),
        cost_estimate=pl.CostEstimate(
            flops=6 * total * width * hidden,
            bytes_accessed=6 * width * hidden,
            transcendentals=total * hidden,
        ),
    )(*theirs, *mine, gate_w, up_w, down_w)


def shift(size, by):
    return [(i, (i + by) % size) for i in range(size)]


def body(moe_in, routes, gates, gate_w, up_w, down_w, queries, latent_cache, lengths):
    rows_here, top_count = routes.shape
    experts = lax.axis_size("x") * lax.axis_size("z")
    columns = lax.axis_size("y")
    width = moe_in.shape[1]
    capacity = 2
    flat_routes = routes.reshape(-1)
    one_hot = (flat_routes[:, None] == jnp.arange(experts, dtype=jnp.int32)[None, :]).astype(
        jnp.int32
    )
    earlier = jnp.cumsum(one_hot, axis=0) - one_hot
    slot_ids = jnp.sum(earlier * one_hot, axis=1)
    targets = (flat_routes * capacity + slot_ids).reshape(rows_here, top_count)
    places = jnp.arange(capacity * experts, dtype=jnp.int32)
    named = targets[:, :, None] == places[None, None, :]
    selector = jnp.sum(named.astype(jnp.float32), axis=1).astype(jnp.bfloat16)
    outgoing = jnp.dot(selector.T, moe_in, preferred_element_type=jnp.float32).astype(jnp.bfloat16)
    outgoing = outgoing.reshape(experts, capacity, width)
    own = lax.all_to_all(outgoing, ("x", "z"), split_axis=0, concat_axis=0, tiled=True)
    own = own.reshape(experts * capacity, width)
    steps = [by for by in (2, 1, 3) if by < columns]
    mine = [own] + [lax.ppermute(own, "y", shift(columns, by)) for by in steps]
    theirs = [lax.ppermute(block, "core", shift(2, 1)) for block in mine]
    part_theirs, part_mine = experts_on(theirs, mine, gate_w, up_w, down_w)
    part_back = lax.ppermute(part_theirs, "core", shift(2, 1))
    summed = [
        (
            part_mine[i * own.shape[0] : (i + 1) * own.shape[0]].astype(jnp.float32)
            + part_back[i * own.shape[0] : (i + 1) * own.shape[0]].astype(jnp.float32)
        ).astype(jnp.bfloat16)
        for i in range(columns)
    ]
    arrived = [
        lax.ppermute(block, "y", shift(columns, -by)) for block, by in zip(summed[1:], steps)
    ]
    total = summed[0].astype(jnp.float32)
    for block in arrived:
        total = total + block.astype(jnp.float32)
    total = total.astype(jnp.bfloat16).reshape(experts, capacity, width)
    returned = lax.all_to_all(total, ("x", "z"), split_axis=0, concat_axis=0, tiled=True)
    attended = attend(queries, latent_cache, lengths)
    weight = jnp.sum(jnp.where(named, gates[:, :, None], 0.0), axis=1)
    high = weight.astype(jnp.bfloat16)
    low = (weight - high.astype(jnp.float32)).astype(jnp.bfloat16)
    returned = returned.reshape(-1, width)
    moe_out = jnp.dot(high, returned, preferred_element_type=jnp.float32) + jnp.dot(
        low, returned, preferred_element_type=jnp.float32
    )
    return (moe_out.astype(jnp.bfloat16), attended)


def solution(mesh):
    devices = mesh.devices
    split = Mesh(devices.reshape(devices.shape[0] // 2, 2, 4, 4), ("y", "core", "x", "z"))
    attn, exp = ("y", "core"), ("x", "z")
    both = attn + exp
    placed = (
        P(both, None),
        P(both, None),
        P(both, None),
        P(exp, None, attn),
        P(exp, None, attn),
        P(exp, attn, None),
        P(both, None, None),
        P(both, None, None),
        P(both),
    )
    return jax.shard_map(
        body,
        mesh=split,
        in_specs=placed,
        out_specs=(P(both, None), P(both, None, None)),
        check_vma=False,
    )
```

```python
import jax
import jax.numpy as jnp
from jax import lax
from jax.experimental import pallas as pl
from jax.experimental.pallas import tpu as pltpu
from jax.sharding import Mesh, PartitionSpec as P

KV = 512
CAP = 2
SLOTS = 32
SCORE_SCALE = 192.0 ** (-0.5)
LOG2_E = 1.4426950408889634
VMEM = pl.BlockSpec(memory_space=pltpu.VMEM)
SMALL = pl.CostEstimate(flops=1000, bytes_accessed=1000, transcendentals=0)


def slot_table(routes, experts):
    rows = routes.shape[1]
    shape = (experts * CAP, rows)
    expert = lax.broadcasted_iota(jnp.int32, shape, 0) // CAP
    first = routes[0:1, :] == expert
    second = routes[1:2, :] == expert
    named = (first | second).astype(jnp.float32)
    before = lax.broadcasted_iota(jnp.int32, (rows, rows), 0)
    after = lax.broadcasted_iota(jnp.int32, (rows, rows), 1)
    earlier = jnp.dot(named, (before < after).astype(jnp.float32), preferred_element_type=jnp.float32)
    slot = (lax.broadcasted_iota(jnp.int32, shape, 0) % CAP).astype(jnp.float32)
    here = (earlier > slot - 0.5) & (earlier < slot + 0.5)
    return first & here, second & here


def send_kernel(routes_ref, rows_ref, out_ref):
    first, second = slot_table(routes_ref[...], out_ref.shape[0] // CAP)
    table = (first | second).astype(jnp.bfloat16)
    out = jnp.dot(table, rows_ref[...], preferred_element_type=jnp.float32)
    out_ref[...] = out.astype(jnp.bfloat16)


def combine_kernel(routes_ref, gates_ref, back_ref, out_ref):
    copies, capacity, width = back_ref.shape
    copies = copies * capacity // SLOTS
    first, second = slot_table(routes_ref[...], SLOTS // CAP)
    weight = jnp.where(first, gates_ref[0:1, :], 0.0) + jnp.where(second, gates_ref[1:2, :], 0.0)
    high = weight.astype(jnp.bfloat16)
    low = (weight - high.astype(jnp.float32)).astype(jnp.bfloat16)
    back = back_ref[...].reshape(copies * SLOTS, width)
    high, low = jnp.concatenate([high] * copies, axis=0), jnp.concatenate([low] * copies, axis=0)
    dims = (((0,), (0,)), ((), ()))
    out = lax.dot_general(high, back, dims, preferred_element_type=jnp.float32)
    out = out + lax.dot_general(low, back, dims, preferred_element_type=jnp.float32)
    out_ref[...] = out.astype(jnp.bfloat16)


def attend_kernel(lengths_ref, queries_ref, cache_ref, *refs):
    weights, out_ref, copies, sems = refs[:3], refs[3], refs[4:7], refs[7]

    def weight_copy(i):
        return pltpu.make_async_copy(weights[i], copies[i], sems.at[i])

    for i in range(3):
        pl.when(pl.program_id(0) == i)(weight_copy(i).start)

    length = lengths_ref[pl.program_id(0)]
    scores = lax.dot_general(
        queries_ref[0], cache_ref[0], (((0,), (0,)), ((), ())), preferred_element_type=jnp.float32
    )
    visible = lax.broadcasted_iota(jnp.int32, scores.shape, 1) < length
    scores = jnp.where(visible, scores, -1e30)
    top = jnp.max(scores, axis=1, keepdims=True)
    probs = jnp.exp2((scores - top) * (SCORE_SCALE * LOG2_E))
    total = jnp.sum(probs, axis=1, keepdims=True)
    out = lax.dot_general(
        probs.astype(jnp.bfloat16),
        cache_ref[0, :KV, :],
        (((1,), (1,)), ((), ())),
        preferred_element_type=jnp.float32,
    )
    out_ref[0] = (out / total).astype(jnp.bfloat16)

    @pl.when(pl.program_id(0) == pl.num_programs(0) - 1)
    def _():
        for i in range(3):
            weight_copy(i).wait()


def attend(queries, latent_cache, lengths, weights):
    rows, heads, width = queries.shape
    context = latent_cache.shape[1]
    in_hbm = [pltpu.with_memory_space_constraint(w, pltpu.HBM) for w in weights]
    cache = pltpu.with_memory_space_constraint(jnp.swapaxes(latent_cache, 1, 2), pltpu.HBM)
    return pl.pallas_call(
        attend_kernel,
        grid=(rows,),
        out_shape=(
            jax.ShapeDtypeStruct((rows, heads, KV), jnp.bfloat16),
            *[pltpu.VMEM(w.shape, w.dtype) for w in weights],
        ),
        in_specs=[
            pl.BlockSpec(memory_space=pltpu.SMEM),
            pl.BlockSpec((1, width, heads), lambda r: (r, 0, 0)),
            pl.BlockSpec((1, width, context), lambda r: (r, 0, 0)),
            *[pl.BlockSpec(memory_space=pl.ANY)] * 3,
        ],
        out_specs=(
            pl.BlockSpec((1, heads, KV), lambda r: (r, 0, 0)),
            *[pl.BlockSpec(memory_space=pl.ANY)] * 3,
        ),
        scratch_shapes=[pltpu.SemaphoreType.DMA((3,))],
        compiler_params=pltpu.CompilerParams(vmem_limit_bytes=16 * 2**20),
        cost_estimate=SMALL,
    )(lengths, jnp.swapaxes(queries, 1, 2), cache, *in_hbm)


STEPS = 7


def expert_kernel(count, *refs):
    blocks, (gate_ref, up_ref, down_ref, mine_ref, *theirs_refs) = refs[:count], refs[count:]
    rows = jnp.concatenate([b[...] for b in blocks], axis=0)
    gate_act = jnp.dot(rows, gate_ref[0], preferred_element_type=jnp.float32)
    up_act = jnp.dot(rows, up_ref[0], preferred_element_type=jnp.float32)
    hidden = (gate_act / (1.0 + jnp.exp(-gate_act)) * up_act).astype(jnp.bfloat16)
    half = hidden.shape[0] // 2
    depth = down_ref.shape[2] // STEPS
    for step in range(STEPS):
        part = pl.ds(step * depth, depth)
        out = jnp.dot(hidden, down_ref[0, :, part], preferred_element_type=jnp.float32)
        out = out.astype(jnp.bfloat16)
        size = half // len(theirs_refs)
        for i, theirs_ref in enumerate(theirs_refs):
            theirs_ref[:, part] = out[i * size : (i + 1) * size]
        mine_ref[:, part] = out[half:]


def experts_on(theirs, mine, gate_w, up_w, down_w):
    rows, width = mine[0].shape
    hidden = gate_w.shape[2]
    mine_out = pltpu.VMEM((len(mine) * rows, width), jnp.bfloat16)
    parts = max(1, len(mine) * rows // SLOTS)
    theirs_out = pltpu.VMEM((SLOTS, width), jnp.bfloat16)
    total = 2 * len(mine) * rows

    def kernel(*refs):
        expert_kernel(2 * len(mine), *refs)

    return pl.pallas_call(
        kernel,
        out_shape=(mine_out,) + (theirs_out,) * parts,
        in_specs=[VMEM] * (2 * len(mine) + 3),
        out_specs=(VMEM,) * (1 + parts),
        compiler_params=pltpu.CompilerParams(vmem_limit_bytes=16 * 2**20),
        cost_estimate=SMALL,
    )(*theirs, *mine, gate_w, up_w, down_w)


def shift(size, by):
    return [(i, (i + by) % size) for i in range(size)]


def add_up(first, *others):
    total = first.astype(jnp.float32)
    for other in others:
        total = total + other.astype(jnp.float32)
    return total.astype(jnp.bfloat16)


def sum_kernel(near_ref, own_back, below_back, above_back, far_ref, far_back_ref, out_ref):
    slots, width = far_ref.shape
    columns = out_ref.shape[0] * CAP // slots
    me = lax.axis_index("y")

    def put(by, block):
        column = lax.rem(me + (columns - by), columns)
        place = pl.ds(column * (slots // CAP), slots // CAP)
        out_ref[place] = block.reshape(slots // CAP, CAP, width)

    for i, (by, back_ref) in enumerate(((0, own_back), (1, below_back), (3, above_back))):
        put(by, add_up(near_ref[pl.ds(i * slots, slots), :], back_ref[...]))
    put(2, add_up(far_ref[...], far_back_ref[...]))


def body(moe_in, routes, gates, gate_w, up_w, down_w, queries, latent_cache, lengths):
    experts = lax.axis_size("x") * lax.axis_size("z")
    columns = lax.axis_size("y")
    width = moe_in.shape[1]
    slots = experts * CAP
    routes, gates = routes.T, gates.T
    flat = jax.ShapeDtypeStruct((slots, width), jnp.bfloat16)
    outgoing = pl.pallas_call(
        send_kernel,
        out_shape=flat,
        in_specs=[VMEM, VMEM],
        out_specs=VMEM,
        compiler_params=pltpu.CompilerParams(vmem_limit_bytes=4 * 2**20),
    )(*[pltpu.with_memory_space_constraint(a, pltpu.HBM) for a in (routes, moe_in)])
    outgoing = outgoing.reshape(experts, CAP, width)
    own = lax.all_to_all(outgoing, ("x", "z"), split_axis=0, concat_axis=0, tiled=True)
    own = own.reshape(slots, width)
    swap = shift(2, 1)
    near = [lax.ppermute(own, "y", shift(columns, by)) for by in (1, 3)]
    own_theirs = lax.ppermute(own, "core", swap)
    attended, *weights = attend(queries, latent_cache, lengths, (gate_w, up_w, down_w))
    *near, attended = lax.optimization_barrier((*near, attended))
    half = slots // 2
    far = [
        lax.ppermute(near[0][:half], "y", shift(columns, 1)),
        lax.ppermute(near[1][half:], "y", shift(columns, 3)),
    ]
    near_theirs = [lax.ppermute(block, "core", swap) for block in near]
    near_out = experts_on([own_theirs] + near_theirs, [own] + near, *weights)
    near_back = [lax.ppermute(block, "core", swap) for block in near_out[1:]]
    far[0], far[1], near_mine = lax.optimization_barrier((*far, near_out[0]))
    far_theirs = [lax.ppermute(block, "core", swap) for block in far]
    far_out = experts_on(far_theirs, far, *weights)
    far_back = lax.ppermute(far_out[1], "core", swap)
    summed = pl.pallas_call(
        sum_kernel,
        out_shape=jax.ShapeDtypeStruct((columns * experts, CAP, width), jnp.bfloat16),
        in_specs=[VMEM] * 6,
        out_specs=VMEM,
        compiler_params=pltpu.CompilerParams(vmem_limit_bytes=16 * 2**20),
        cost_estimate=SMALL,
    )(near_mine, *near_back, far_out[0], far_back)
    returned = lax.all_to_all(summed, ("y", "x", "z"), split_axis=0, concat_axis=0, tiled=True)
    moe_out = pl.pallas_call(
        combine_kernel,
        out_shape=jax.ShapeDtypeStruct(moe_in.shape, jnp.bfloat16),
        in_specs=[VMEM, VMEM, VMEM],
        out_specs=VMEM,
        compiler_params=pltpu.CompilerParams(vmem_limit_bytes=4 * 2**20),
    )(routes, gates, returned)
    return (moe_out, attended)


def solution(mesh):
    devices = mesh.devices
    split = Mesh(devices.reshape(devices.shape[0] // 2, 2, 4, 4), ("y", "core", "x", "z"))
    attn, exp = ("y", "core"), ("x", "z")
    both = attn + exp
    placed = (
        P(both, None),
        P(both, None),
        P(both, None),
        P(exp, None, attn),
        P(exp, None, attn),
        P(exp, attn, None),
        P(both, None, None),
        P(both, None, None),
        P(both),
    )
    return jax.shard_map(
        body,
        mesh=split,
        in_specs=placed,
        out_specs=(P(both, None), P(both, None, None)),
        check_vma=False,
    )
```

```python
import functools

import jax
import jax.numpy as jnp
from jax import lax
from jax.experimental import pallas as pl
from jax.experimental.pallas import tpu as pltpu
from jax.sharding import Mesh, PartitionSpec as P

KV = 512
CAP = 2
SLOTS = 32
SCORE_SCALE = 192.0 ** (-0.5)
LOG2_E = 1.4426950408889634
VMEM = pl.BlockSpec(memory_space=pltpu.VMEM)
SMALL = pl.CostEstimate(flops=1000, bytes_accessed=1000, transcendentals=0)


def slot_table(routes, experts):
    rows = routes.shape[1]
    shape = (experts * CAP, rows)
    expert = lax.broadcasted_iota(jnp.int32, shape, 0) // CAP
    first = routes[0:1, :] == expert
    second = routes[1:2, :] == expert
    named = (first | second).astype(jnp.float32)
    before = lax.broadcasted_iota(jnp.int32, (rows, rows), 0)
    after = lax.broadcasted_iota(jnp.int32, (rows, rows), 1)
    earlier = jnp.dot(named, (before < after).astype(jnp.float32), preferred_element_type=jnp.float32)
    slot = (lax.broadcasted_iota(jnp.int32, shape, 0) % CAP).astype(jnp.float32)
    here = (earlier > slot - 0.5) & (earlier < slot + 0.5)
    return first & here, second & here


def send_kernel(routes_ref, rows_ref, out_ref):
    first, second = slot_table(routes_ref[...], out_ref.shape[0] // CAP)
    table = (first | second).astype(jnp.bfloat16)
    out = jnp.dot(table, rows_ref[...], preferred_element_type=jnp.float32)
    out_ref[...] = out.astype(jnp.bfloat16)


def combine_kernel(routes_ref, gates_ref, back_ref, out_ref):
    copies, capacity, width = back_ref.shape
    copies = copies * capacity // SLOTS
    first, second = slot_table(routes_ref[...], SLOTS // CAP)
    weight = jnp.where(first, gates_ref[0:1, :], 0.0) + jnp.where(second, gates_ref[1:2, :], 0.0)
    high = weight.astype(jnp.bfloat16)
    low = (weight - high.astype(jnp.float32)).astype(jnp.bfloat16)
    back = back_ref[...].reshape(copies * SLOTS, width)
    high, low = jnp.concatenate([high] * copies, axis=0), jnp.concatenate([low] * copies, axis=0)
    dims = (((0,), (0,)), ((), ()))
    out = lax.dot_general(high, back, dims, preferred_element_type=jnp.float32)
    out = out + lax.dot_general(low, back, dims, preferred_element_type=jnp.float32)
    out_ref[...] = out.astype(jnp.bfloat16)


PIECES = 4


def attend_kernel(lengths_ref, queries_ref, cache_hbm, out_ref, cache_ref, sems):
    rows, _, context = cache_ref.shape
    size = context // PIECES

    def for_pieces(row, act):
        for piece in range(PIECES):
            part = pl.ds(piece * size, size)
            copy = pltpu.make_async_copy(
                cache_hbm.at[row, :, part], cache_ref.at[row, :, part], sems.at[row, piece]
            )
            pl.when(lengths_ref[row] > piece * size)(functools.partial(act, copy))

    def attend_to(row, length, most):
        scores = lax.dot_general(
            queries_ref[row],
            cache_ref[row, :, :most],
            (((0,), (0,)), ((), ())),
            preferred_element_type=jnp.float32,
        )
        visible = lax.broadcasted_iota(jnp.int32, scores.shape, 1) < length
        scores = jnp.where(visible, scores, -1e30)
        top = jnp.max(scores, axis=1, keepdims=True)
        probs = jnp.exp2((scores - top) * (SCORE_SCALE * LOG2_E))
        total = jnp.sum(probs, axis=1, keepdims=True)
        out = lax.dot_general(
            probs.astype(jnp.bfloat16),
            cache_ref[row, :KV, :most],
            (((1,), (1,)), ((), ())),
            preferred_element_type=jnp.float32,
        )
        out_ref[row] = (out / total).astype(jnp.bfloat16)

    for row in range(rows):
        for_pieces(row, lambda copy: copy.start())

    @pl.loop(0, rows)
    def _(row):
        length = lengths_ref[row]
        for_pieces(row, lambda copy: copy.wait())
        for piece in range(PIECES):
            here = (length > piece * size) & (length <= (piece + 1) * size)
            pl.when(here)(functools.partial(attend_to, row, length, (piece + 1) * size))


def attend(queries, latent_cache, lengths):
    rows, heads, width = queries.shape
    context = latent_cache.shape[1]
    cache = pltpu.with_memory_space_constraint(jnp.swapaxes(latent_cache, 1, 2), pltpu.HBM)
    return pl.pallas_call(
        attend_kernel,
        out_shape=jax.ShapeDtypeStruct((rows, heads, KV), jnp.bfloat16),
        in_specs=[
            pl.BlockSpec(memory_space=pltpu.SMEM),
            VMEM,
            pl.BlockSpec(memory_space=pl.ANY),
        ],
        out_specs=VMEM,
        scratch_shapes=[
            pltpu.VMEM((rows, width, context), jnp.bfloat16),
            pltpu.SemaphoreType.DMA((rows, PIECES)),
        ],
        compiler_params=pltpu.CompilerParams(vmem_limit_bytes=20 * 2**20),
        cost_estimate=SMALL,
    )(lengths, jnp.swapaxes(queries, 1, 2), cache)


STEPS = 7


def expert_kernel(count, *refs):
    blocks, (gate_ref, up_ref, down_ref, mine_ref, *theirs_refs) = refs[:count], refs[count:]
    rows = jnp.concatenate([b[...] for b in blocks], axis=0)
    gate_act = jnp.dot(rows, gate_ref[0], preferred_element_type=jnp.float32)
    up_act = jnp.dot(rows, up_ref[0], preferred_element_type=jnp.float32)
    hidden = (gate_act / (1.0 + jnp.exp(-gate_act)) * up_act).astype(jnp.bfloat16)
    half = hidden.shape[0] // 2
    depth = down_ref.shape[2] // STEPS
    for step in range(STEPS):
        part = pl.ds(step * depth, depth)
        out = jnp.dot(hidden, down_ref[0, :, part], preferred_element_type=jnp.float32)
        out = out.astype(jnp.bfloat16)
        size = half // len(theirs_refs)
        for i, theirs_ref in enumerate(theirs_refs):
            theirs_ref[:, part] = out[i * size : (i + 1) * size]
        mine_ref[:, part] = out[half:]


def experts_on(theirs, mine, gate_w, up_w, down_w):
    width, hidden = gate_w.shape[1:]
    rows = sum(block.shape[0] for block in mine)
    mine_out = pltpu.VMEM((rows, width), jnp.bfloat16)
    parts = rows // SLOTS
    theirs_out = pltpu.VMEM((SLOTS, width), jnp.bfloat16)

    def kernel(*refs):
        expert_kernel(len(theirs) + len(mine), *refs)

    return pl.pallas_call(
        kernel,
        out_shape=(mine_out,) + (theirs_out,) * parts,
        in_specs=[VMEM] * (len(theirs) + len(mine) + 3),
        out_specs=(VMEM,) * (1 + parts),
        compiler_params=pltpu.CompilerParams(vmem_limit_bytes=16 * 2**20),
        cost_estimate=SMALL,
    )(*theirs, *mine, gate_w, up_w, down_w)


def shift(size, by):
    return [(i, (i + by) % size) for i in range(size)]


def add_up(first, *others):
    total = first.astype(jnp.float32)
    for other in others:
        total = total + other.astype(jnp.float32)
    return total.astype(jnp.bfloat16)


def sum_kernel(near_ref, own_back, first_back, second_back, far_ref, far_back_ref, out_ref):
    slots, width = far_ref.shape
    columns = out_ref.shape[0] * CAP // slots
    me = lax.axis_index("y")

    def put(by, block):
        column = lax.rem(me + (columns - by), columns)
        place = pl.ds(column * (slots // CAP), slots // CAP)
        out_ref[place] = block.reshape(slots // CAP, CAP, width)

    core = lax.axis_index("core")
    backs = ((0, own_back), (1 + 2 * core, first_back), (3 - 2 * core, second_back))
    for i, (by, back_ref) in enumerate(backs):
        put(by, add_up(near_ref[pl.ds(i * slots, slots), :], back_ref[...]))
    put(2, add_up(far_ref[...], far_back_ref[...]))


def body(moe_in, routes, gates, gate_w, up_w, down_w, queries, latent_cache, lengths):
    experts = lax.axis_size("x") * lax.axis_size("z")
    columns = lax.axis_size("y")
    width = moe_in.shape[1]
    slots = experts * CAP
    routes, gates = routes.T, gates.T
    flat = jax.ShapeDtypeStruct((slots, width), jnp.bfloat16)
    outgoing = pl.pallas_call(
        send_kernel,
        out_shape=flat,
        in_specs=[VMEM, VMEM],
        out_specs=VMEM,
        compiler_params=pltpu.CompilerParams(vmem_limit_bytes=4 * 2**20),
    )(*[pltpu.with_memory_space_constraint(a, pltpu.HBM) for a in (routes, moe_in)])
    outgoing = outgoing.reshape(experts, CAP, width)
    own = lax.all_to_all(outgoing, ("x", "z"), split_axis=0, concat_axis=0, tiled=True)
    own = own.reshape(slots, width)
    swap = shift(2, 1)
    both = ("y", "core")
    one_way = [(2 * y + c, 2 * ((y + 1 - 2 * c) % columns) + c) for y in range(columns) for c in (0, 1)]
    other_way = [(there, here) for here, there in one_way]
    first = lax.ppermute(own, both, one_way)
    second = lax.ppermute(own, both, other_way)
    own_theirs = lax.ppermute(own, "core", swap)
    attended = attend(queries, latent_cache, lengths)
    weights = [pltpu.with_memory_space_constraint(w, pltpu.VMEM) for w in (gate_w, up_w, down_w)]
    first, second, attended = lax.optimization_barrier((first, second, attended))
    far = lax.ppermute(first, both, one_way)
    near = [first, second]
    near_theirs = [lax.ppermute(block, "core", swap) for block in near]
    near_out = experts_on([own_theirs] + near_theirs, [own] + near, *weights)
    near_back = [lax.ppermute(block, "core", swap) for block in near_out[1:]]
    far, near_mine = lax.optimization_barrier((far, near_out[0]))
    far_out = experts_on([lax.ppermute(far, "core", swap)], [far], *weights)
    far_back = lax.ppermute(far_out[1], "core", swap)
    summed = pl.pallas_call(
        sum_kernel,
        out_shape=jax.ShapeDtypeStruct((columns * experts, CAP, width), jnp.bfloat16),
        in_specs=[VMEM] * 6,
        out_specs=VMEM,
        compiler_params=pltpu.CompilerParams(vmem_limit_bytes=16 * 2**20),
        cost_estimate=SMALL,
    )(near_mine, *near_back, far_out[0], far_back)
    returned = lax.all_to_all(summed, ("y", "x", "z"), split_axis=0, concat_axis=0, tiled=True)
    moe_out = pl.pallas_call(
        combine_kernel,
        out_shape=jax.ShapeDtypeStruct(moe_in.shape, jnp.bfloat16),
        in_specs=[VMEM, VMEM, VMEM],
        out_specs=VMEM,
        compiler_params=pltpu.CompilerParams(vmem_limit_bytes=4 * 2**20),
    )(routes, gates, returned)
    return (moe_out, attended)


def solution(mesh):
    devices = mesh.devices
    split = Mesh(devices.reshape(devices.shape[0] // 2, 2, 4, 4), ("y", "core", "x", "z"))
    attn, exp = ("y", "core"), ("x", "z")
    both = attn + exp
    placed = (
        P(both, None),
        P(both, None),
        P(both, None),
        P(exp, None, attn),
        P(exp, None, attn),
        P(exp, attn, None),
        P(both, None, None),
        P(both, None, None),
        P(both),
    )
    return jax.shard_map(
        body,
        mesh=split,
        in_specs=placed,
        out_specs=(P(both, None), P(both, None, None)),
        check_vma=False,
    )
```

```python
import functools

import jax
import jax.numpy as jnp
from jax import lax
from jax.experimental import pallas as pl
from jax.experimental.pallas import tpu as pltpu
from jax.sharding import Mesh, PartitionSpec as P

KV = 512
CAP = 2
SLOTS = 32
SCORE_SCALE = 192.0 ** (-0.5)
LOG2_E = 1.4426950408889634
VMEM = pl.BlockSpec(memory_space=pltpu.VMEM)
SMALL = pl.CostEstimate(flops=1000, bytes_accessed=1000, transcendentals=0)


def slot_table(routes, experts):
    rows = routes.shape[1]
    shape = (experts * CAP, rows)
    expert = lax.broadcasted_iota(jnp.int32, shape, 0) // CAP
    first = routes[0:1, :] == expert
    second = routes[1:2, :] == expert
    named = (first | second).astype(jnp.float32)
    before = lax.broadcasted_iota(jnp.int32, (rows, rows), 0)
    after = lax.broadcasted_iota(jnp.int32, (rows, rows), 1)
    earlier = jnp.dot(named, (before < after).astype(jnp.float32), preferred_element_type=jnp.float32)
    slot = (lax.broadcasted_iota(jnp.int32, shape, 0) % CAP).astype(jnp.float32)
    here = (earlier > slot - 0.5) & (earlier < slot + 0.5)
    return first & here, second & here


def send_kernel(routes_ref, rows_ref, out_ref):
    first, second = slot_table(routes_ref[...], out_ref.shape[0] // CAP)
    table = (first | second).astype(jnp.bfloat16)
    out = jnp.dot(table, rows_ref[...], preferred_element_type=jnp.float32)
    out_ref[...] = out.astype(jnp.bfloat16)


def combine_kernel(routes_ref, gates_ref, back_ref, out_ref):
    copies, capacity, width = back_ref.shape
    copies = copies * capacity // SLOTS
    first, second = slot_table(routes_ref[...], SLOTS // CAP)
    weight = jnp.where(first, gates_ref[0:1, :], 0.0) + jnp.where(second, gates_ref[1:2, :], 0.0)
    rows = weight.shape[1]
    weight = jnp.concatenate([weight, jnp.zeros((SLOTS, 8 - rows % 8), jnp.float32)], axis=1)
    high = weight.astype(jnp.bfloat16)
    low = (weight - high.astype(jnp.float32)).astype(jnp.bfloat16)
    parts = jnp.concatenate([jnp.concatenate([high, low], axis=1)] * copies, axis=0)
    size = width // STEPS
    for step in range(STEPS):
        part = pl.ds(step * size, size)
        back = back_ref[:, :, part].reshape(copies * SLOTS, size)
        out = lax.dot_general(
            parts, back, (((0,), (0,)), ((), ())), preferred_element_type=jnp.float32
        )
        out = out[: weight.shape[1]] + out[weight.shape[1] :]
        out_ref[:, part] = out[:rows].astype(jnp.bfloat16)


PIECES = 4


def attend_kernel(lengths_ref, queries_ref, cache_hbm, out_ref, cache_ref, sems):
    rows, _, context = cache_ref.shape
    size = context // PIECES

    def for_pieces(row, act):
        for piece in range(PIECES):
            part = pl.ds(piece * size, size)
            copy = pltpu.make_async_copy(
                cache_hbm.at[row, :, part], cache_ref.at[row, :, part], sems.at[row, piece]
            )
            pl.when(lengths_ref[row] > piece * size)(functools.partial(act, copy))

    def attend_to(row, length, most):
        scores = lax.dot_general(
            queries_ref[row],
            cache_ref[row, :, :most],
            (((0,), (0,)), ((), ())),
            preferred_element_type=jnp.float32,
        )
        visible = lax.broadcasted_iota(jnp.int32, scores.shape, 1) < length
        scores = jnp.where(visible, scores, -1e30)
        top = jnp.max(scores, axis=1, keepdims=True)
        probs = jnp.exp2((scores - top) * (SCORE_SCALE * LOG2_E))
        total = jnp.sum(probs, axis=1, keepdims=True)
        out = lax.dot_general(
            probs.astype(jnp.bfloat16),
            cache_ref[row, :KV, :most],
            (((1,), (1,)), ((), ())),
            preferred_element_type=jnp.float32,
        )
        out_ref[row] = (out / total).astype(jnp.bfloat16)

    for row in range(rows):
        for_pieces(row, lambda copy: copy.start())

    @pl.loop(0, rows)
    def _(row):
        length = lengths_ref[row]
        for_pieces(row, lambda copy: copy.wait())
        for piece in range(PIECES):
            here = (length > piece * size) & (length <= (piece + 1) * size)
            pl.when(here)(functools.partial(attend_to, row, length, (piece + 1) * size))


def attend(queries, latent_cache, lengths):
    rows, heads, width = queries.shape
    context = latent_cache.shape[1]
    cache = pltpu.with_memory_space_constraint(jnp.swapaxes(latent_cache, 1, 2), pltpu.HBM)
    return pl.pallas_call(
        attend_kernel,
        out_shape=jax.ShapeDtypeStruct((rows, heads, KV), jnp.bfloat16),
        in_specs=[
            pl.BlockSpec(memory_space=pltpu.SMEM),
            VMEM,
            pl.BlockSpec(memory_space=pl.ANY),
        ],
        out_specs=VMEM,
        scratch_shapes=[
            pltpu.VMEM((rows, width, context), jnp.bfloat16),
            pltpu.SemaphoreType.DMA((rows, PIECES)),
        ],
        compiler_params=pltpu.CompilerParams(vmem_limit_bytes=20 * 2**20),
        cost_estimate=SMALL,
    )(lengths, jnp.swapaxes(queries, 1, 2), cache)


STEPS = 7


def expert_kernel(count, *refs):
    blocks, (gate_ref, up_ref, down_ref, mine_ref, *theirs_refs) = refs[:count], refs[count:]
    rows = jnp.concatenate([b[...] for b in blocks], axis=0)
    gate_act = jnp.dot(rows, gate_ref[0], preferred_element_type=jnp.float32)
    up_act = jnp.dot(rows, up_ref[0], preferred_element_type=jnp.float32)
    hidden = (gate_act / (1.0 + jnp.exp(-gate_act)) * up_act).astype(jnp.bfloat16)
    half = hidden.shape[0] // 2
    depth = down_ref.shape[2] // STEPS
    for step in range(STEPS):
        part = pl.ds(step * depth, depth)
        out = jnp.dot(hidden, down_ref[0, :, part], preferred_element_type=jnp.float32)
        out = out.astype(jnp.bfloat16)
        size = half // len(theirs_refs)
        for i, theirs_ref in enumerate(theirs_refs):
            theirs_ref[:, part] = out[i * size : (i + 1) * size]
        mine_ref[:, part] = out[half:]


def experts_on(theirs, mine, gate_w, up_w, down_w):
    width, hidden = gate_w.shape[1:]
    rows = sum(block.shape[0] for block in mine)
    mine_out = pltpu.VMEM((rows, width), jnp.bfloat16)
    parts = rows // SLOTS
    theirs_out = pltpu.VMEM((SLOTS, width), jnp.bfloat16)

    def kernel(*refs):
        expert_kernel(len(theirs) + len(mine), *refs)

    return pl.pallas_call(
        kernel,
        out_shape=(mine_out,) + (theirs_out,) * parts,
        in_specs=[VMEM] * (len(theirs) + len(mine) + 3),
        out_specs=(VMEM,) * (1 + parts),
        compiler_params=pltpu.CompilerParams(vmem_limit_bytes=16 * 2**20),
        cost_estimate=SMALL,
    )(*theirs, *mine, gate_w, up_w, down_w)


def shift(size, by):
    return [(i, (i + by) % size) for i in range(size)]


def add_up(first, *others):
    total = first.astype(jnp.float32)
    for other in others:
        total = total + other.astype(jnp.float32)
    return total.astype(jnp.bfloat16)


def sum_kernel(near_ref, own_back, first_back, second_back, far_ref, far_back_ref, out_ref):
    slots, width = far_ref.shape
    columns = out_ref.shape[0] * CAP // slots
    me = lax.axis_index("y")

    def put(by, block):
        column = lax.rem(me + (columns - by), columns)
        place = pl.ds(column * (slots // CAP), slots // CAP)
        out_ref[place] = block.reshape(slots // CAP, CAP, width)

    core = lax.axis_index("core")
    backs = ((0, own_back), (1 + 2 * core, first_back), (3 - 2 * core, second_back))
    for i, (by, back_ref) in enumerate(backs):
        put(by, add_up(near_ref[pl.ds(i * slots, slots), :], back_ref[...]))
    put(2, add_up(far_ref[...], far_back_ref[...]))


def body(moe_in, routes, gates, gate_w, up_w, down_w, queries, latent_cache, lengths):
    experts = lax.axis_size("x") * lax.axis_size("z")
    columns = lax.axis_size("y")
    width = moe_in.shape[1]
    slots = experts * CAP
    routes, gates = routes.T, gates.T
    flat = jax.ShapeDtypeStruct((slots, width), jnp.bfloat16)
    outgoing = pl.pallas_call(
        send_kernel,
        out_shape=flat,
        in_specs=[VMEM, VMEM],
        out_specs=VMEM,
        compiler_params=pltpu.CompilerParams(vmem_limit_bytes=4 * 2**20),
    )(*[pltpu.with_memory_space_constraint(a, pltpu.HBM) for a in (routes, moe_in)])
    outgoing = outgoing.reshape(experts, CAP, width)
    own = lax.all_to_all(outgoing, ("x", "z"), split_axis=0, concat_axis=0, tiled=True)
    own = own.reshape(slots, width)
    swap = shift(2, 1)
    both = ("y", "core")
    one_way = [(2 * y + c, 2 * ((y + 1 - 2 * c) % columns) + c) for y in range(columns) for c in (0, 1)]
    other_way = [(there, here) for here, there in one_way]
    first = lax.ppermute(own, both, one_way)
    second = lax.ppermute(own, both, other_way)
    own_theirs = lax.ppermute(own, "core", swap)
    attended = attend(queries, latent_cache, lengths)
    weights = [pltpu.with_memory_space_constraint(w, pltpu.VMEM) for w in (gate_w, up_w, down_w)]
    first, second, attended = lax.optimization_barrier((first, second, attended))
    far = lax.ppermute(first, both, one_way)
    near = [first, second]
    half = slots // 2
    near_theirs = [
        lax.ppermute(block[i : i + half], "core", swap) for block in near for i in (0, half)
    ]
    near_out = experts_on([own_theirs] + near_theirs, [own] + near, *weights)
    near_back = [lax.ppermute(block, "core", swap) for block in near_out[1:]]
    far, near_mine = lax.optimization_barrier((far, near_out[0]))
    far_out = experts_on([lax.ppermute(far, "core", swap)], [far], *weights)
    far_back = lax.ppermute(far_out[1], "core", swap)
    summed = pl.pallas_call(
        sum_kernel,
        out_shape=jax.ShapeDtypeStruct((columns * experts, CAP, width), jnp.bfloat16),
        in_specs=[VMEM] * 6,
        out_specs=VMEM,
        compiler_params=pltpu.CompilerParams(vmem_limit_bytes=16 * 2**20),
        cost_estimate=SMALL,
    )(near_mine, *near_back, far_out[0], far_back)
    returned = lax.all_to_all(summed, ("y", "x", "z"), split_axis=0, concat_axis=0, tiled=True)
    moe_out = pl.pallas_call(
        combine_kernel,
        out_shape=jax.ShapeDtypeStruct(moe_in.shape, jnp.bfloat16),
        in_specs=[VMEM, VMEM, VMEM],
        out_specs=VMEM,
        compiler_params=pltpu.CompilerParams(vmem_limit_bytes=4 * 2**20),
    )(*[pltpu.with_memory_space_constraint(a, pltpu.VMEM) for a in (routes, gates)], returned)
    return (moe_out, attended)


def solution(mesh):
    devices = mesh.devices
    split = Mesh(devices.reshape(devices.shape[0] // 2, 2, 4, 4), ("y", "core", "x", "z"))
    attn, exp = ("y", "core"), ("x", "z")
    both = attn + exp
    placed = (
        P(both, None),
        P(both, None),
        P(both, None),
        P(exp, None, attn),
        P(exp, None, attn),
        P(exp, attn, None),
        P(both, None, None),
        P(both, None, None),
        P(both),
    )
    return jax.shard_map(
        body,
        mesh=split,
        in_specs=placed,
        out_specs=(P(both, None), P(both, None, None)),
        check_vma=False,
    )
```
